512 devices in a mesh: dom: 16 (over z, core), pencil: 32 (over x, y).
Axes of the slice: x: 4, y: 8, z: 8, core: 2. Of those that a mesh axis runs over, the one named last changes fastest.
Arguments:
- modes_now: float32 [16, 128, 512, 128], P('dom', 'pencil'), may hold values from -6 to 6
- modes_prev: float32 [16, 128, 512, 128], P('dom', 'pencil'), may hold values from -6 to 6
- extents: int32 [16], P('dom'), may hold values from 64 to 128, as said below
Outputs:
- pressure: float32 [16, 512, 128, 128], P('dom', 'pencil')
- modes_next: float32 [16, 128, 512, 128], P('dom', 'pencil')
The draws below stay inside these ranges and needn't reach their ends.
Inputs may be any that keep to these rules, and one draw needn't show every extreme that they name: `extents`: some partition has exactly 128 live cells along x.
All inputs are finite; a program needn't handle non-finite values.
Results may differ from the reference program's by a relative error of at most 0.0003.
Values sent between devices are 32-bit elements; how exact they have to be, the bound alone decides.
A program may use at most 64 MiB of HBM per device.

```python
import jax
import jax.numpy as jnp
from jax import lax

GX = 128
GY = 128
GZ = 512
NPART = 16


def draw_extents(key, part):
    key = jax.random.fold_in(key, 7)
    draw_key, pick_key = jax.random.split(key)
    spans = jax.random.randint(draw_key, (NPART,), GX // 2, GX + 1)
    chosen = jax.random.randint(pick_key, (), 0, NPART)
    return jnp.where(jnp.arange(NPART) == chosen, GX, spans).astype(jnp.int32)


def block_levels(own_key, shape, shards, smallest, high):
    level, own = 1.0, jax.random.fold_in(own_key, 6)
    for position, blocks in shards:
        steps = jnp.exp(jax.random.uniform(jax.random.fold_in(own, position), (blocks,), jnp.float32, smallest / len(shards), high / len(shards)))
        level = level * jnp.repeat(steps, shape[position] // blocks).reshape([-1 if axis == position else 1 for axis in range(len(shape))])
    return level


def centred(rng, dims, deviation, bound, cuts=(), held_as=jnp.bfloat16):
    factor_of = block_levels(rng, dims, cuts, -0.22, 0.18) if cuts else 1.0
    drawn = jax.random.normal(rng, dims, jnp.float32) * deviation * factor_of
    return jnp.minimum(jnp.maximum(drawn, -bound), bound).astype(held_as)


def setup_inputs(seed: int = 0) -> dict:
    splits = jax.random.split(jax.random.key(seed), 4)
    modes_now = centred(splits[0], (NPART, GY, GZ, GX), 1.0, 6.0, ((0, 16), (1, 32)), jnp.float32)
    modes_prev = centred(splits[1], (NPART, GY, GZ, GX), 1.0, 6.0, ((0, 16), (1, 32)), jnp.float32)
    extents = draw_extents(jax.random.fold_in(splits[3], 71), 0)
    return dict(modes_now=modes_now, modes_prev=modes_prev, extents=extents)


HIGH = lax.Precision.HIGHEST
COEF_ONE = 1.5
COEF_TWO = -0.15
COEF_THREE = 1.0 / 90.0
STEP_DT = 0.5

def cosine_table(live, size):
    live = jnp.asarray(live, jnp.int32)
    mode_index = lax.broadcasted_iota(jnp.int32, (size, size), 0)
    cell_index = lax.broadcasted_iota(jnp.int32, (size, size), 1)
    phase_index = mode_index * (2 * cell_index + 1) % (4 * live)
    count = live.astype(jnp.float32)
    radians = jnp.pi * phase_index.astype(jnp.float32) / (2.0 * count)
    norm_factor = jnp.where(mode_index == 0, jnp.sqrt(1.0 / count), jnp.sqrt(2.0 / count))
    inside = (mode_index < live) & (cell_index < live)
    return jnp.where(inside, norm_factor * jnp.cos(radians), jnp.float32(0.0))

def layer_table(live, size, positions):
    live = jnp.asarray(live, jnp.int32)
    mode_index = lax.broadcasted_iota(jnp.int32, (size, 6), 0)
    phase_index = mode_index * (2 * positions[None, :] + 1) % (4 * live)
    count = live.astype(jnp.float32)
    radians = jnp.pi * phase_index.astype(jnp.float32) / (2.0 * count)
    norm_factor = jnp.where(mode_index == 0, jnp.sqrt(1.0 / count), jnp.sqrt(2.0 / count))
    return jnp.where(mode_index < live, norm_factor * jnp.cos(radians), jnp.float32(0.0))

def face_forcing(own, other):
    diff = other - own
    first_layer = COEF_ONE * diff[..., 0, :, :] + COEF_TWO * diff[..., 1, :, :] + COEF_THREE * diff[..., 2, :, :]
    second_layer = COEF_TWO * diff[..., 0, :, :] + COEF_THREE * diff[..., 1, :, :]
    third_layer = COEF_THREE * diff[..., 0, :, :]
    return jnp.stack([first_layer, second_layer, third_layer], axis=-3)

def advance_modes(modes, earlier, forcing, extent, ky_start, size_y, size_z):
    shape = modes.shape
    mode_y = (ky_start + lax.broadcasted_iota(jnp.int32, shape, 0)).astype(jnp.float32)
    mode_z = lax.broadcasted_iota(jnp.int32, shape, 1).astype(jnp.float32)
    mode_x_int = lax.broadcasted_iota(jnp.int32, shape, 2)
    mode_x = mode_x_int.astype(jnp.float32)
    frequency = jnp.pi * jnp.sqrt((mode_x / extent.astype(jnp.float32)) ** 2 + (mode_y / size_y) ** 2 + (mode_z / size_z) ** 2)
    gain_force = STEP_DT * STEP_DT * jnp.sinc(frequency * STEP_DT / (2.0 * jnp.pi)) ** 2
    advanced = 2.0 * jnp.cos(frequency * STEP_DT) * modes - earlier + gain_force * forcing
    return jnp.where(mode_x_int < extent, advanced, jnp.float32(0.0))

def reference(modes_now, modes_prev, extents):
    table_z = cosine_table(GZ, GZ)
    table_y = cosine_table(GY, GY)

    def to_field(inputs):
        modes, extent = inputs
        table_x = cosine_table(extent, GX)
        along_z = jnp.einsum('bck,cz->bzk', modes, table_z, precision=HIGH)
        along_y = jnp.einsum('bzk,by->zyk', along_z, table_y, precision=HIGH)
        return jnp.einsum('zyk,kx->zyx', along_y, table_x, precision=HIGH)
    pressure = lax.map(to_field, (modes_now, extents))
    lower_rim = jnp.moveaxis(pressure[:, :, :, 0:3], 3, 1)

    def upper_layers(inputs):
        field, extent = inputs
        block = lax.dynamic_slice_in_dim(field, (extent - 3).astype(jnp.int32), 3, axis=2)
        return jnp.moveaxis(block, 2, 0)[::-1]
    upper_rim = lax.map(upper_layers, (pressure, extents))
    nothing = jnp.zeros_like(lower_rim[:1])
    from_lower = jnp.concatenate([nothing, upper_rim[:-1]], axis=0)
    from_upper = jnp.concatenate([lower_rim[1:], nothing], axis=0)
    domain = jnp.arange(NPART, dtype=jnp.int32)
    lower_force = face_forcing(lower_rim, from_lower) * (domain > 0).astype(jnp.float32)[:, None, None, None]
    upper_force = face_forcing(upper_rim, from_upper) * (domain < NPART - 1).astype(jnp.float32)[:, None, None, None]
    layers = jnp.concatenate([lower_force, upper_force], axis=1)

    def step_modes(inputs):
        modes, earlier, layer_block, extent = inputs
        offsets = jnp.arange(3, dtype=jnp.int32)
        positions = jnp.concatenate([offsets, extent - 1 - offsets]).astype(jnp.int32)
        layer_cols = layer_table(extent, GX, positions)
        partial_value = jnp.einsum('lzy,by->lbz', layer_block, table_y, precision=HIGH)
        partial_value = jnp.einsum('lbz,cz->lbc', partial_value, table_z, precision=HIGH)
        forcing = jnp.einsum('lbc,kl->bck', partial_value, layer_cols, precision=HIGH)
        return advance_modes(modes, earlier, forcing, extent, 0, GY, GZ)
    modes_next = lax.map(step_modes, (modes_now, modes_prev, layers, extents))
    return (pressure, modes_next)
```

```python
import jax
import jax.numpy as jnp
from jax import lax
from jax.sharding import PartitionSpec as P

HIGH = lax.Precision.HIGHEST
COEF_ONE = 1.5
COEF_TWO = -0.15
COEF_THREE = 1.0 / 90.0
STEP_DT = 0.5
SINC_SERIES = (1.0, -1.0 / 6, 1.0 / 120, -1.0 / 5040, 1.0 / 362880, -1.0 / 39916800, 1.0 / 6227020800, -1.0 / 1307674368000)


def from_behind(block, axis, distance):
    devices = range(lax.axis_size(axis))
    route = [(i - distance, i) for i in devices if i - distance in devices]
    return lax.ppermute(block, axis, route)


def cosine_table(live, size):
    live = jnp.asarray(live, jnp.int32)
    mode_index = lax.broadcasted_iota(jnp.int32, (size, size), 0)
    cell_index = lax.broadcasted_iota(jnp.int32, (size, size), 1)
    phase_index = mode_index * (2 * cell_index + 1) % (4 * live)
    count = live.astype(jnp.float32)
    radians = jnp.pi * phase_index.astype(jnp.float32) / (2.0 * count)
    norm_factor = jnp.where(mode_index == 0, jnp.sqrt(1.0 / count), jnp.sqrt(2.0 / count))
    inside = (mode_index < live) & (cell_index < live)
    return jnp.where(inside, norm_factor * jnp.cos(radians), jnp.float32(0.0))


def face_forcing(own, other):
    diff = other - own
    first_layer = (
        COEF_ONE * diff[..., 0, :, :]
        + COEF_TWO * diff[..., 1, :, :]
        + COEF_THREE * diff[..., 2, :, :]
    )
    second_layer = COEF_TWO * diff[..., 0, :, :] + COEF_THREE * diff[..., 1, :, :]
    third_layer = COEF_THREE * diff[..., 0, :, :]
    return jnp.stack([first_layer, second_layer, third_layer], axis=-3)


def advance_modes(modes, earlier, forcing, extent, ky_start, size_y, size_z):
    shape = modes.shape
    mode_y = (ky_start + lax.broadcasted_iota(jnp.int32, shape, 0)).astype(jnp.float32)
    mode_z = lax.broadcasted_iota(jnp.int32, shape, 1).astype(jnp.float32)
    mode_x_int = lax.broadcasted_iota(jnp.int32, shape, 2)
    mode_x = mode_x_int.astype(jnp.float32)
    half = jnp.pi * STEP_DT / 2.0
    square = half * half * (
        (mode_x / extent.astype(jnp.float32)) ** 2 + (mode_y / size_y) ** 2 + (mode_z / size_z) ** 2
    )
    series = jnp.float32(SINC_SERIES[-1])
    for term in SINC_SERIES[-2::-1]:
        series = series * square + jnp.float32(term)
    gain = series * series
    advanced = 2.0 * modes - earlier + gain * (STEP_DT * STEP_DT * forcing - 4.0 * square * modes)
    return jnp.where(mode_x_int < extent, advanced, jnp.float32(0.0))


def face_columns(live, size):
    offsets = jnp.arange(3, dtype=jnp.int32)
    cells = jnp.concatenate([offsets, live - 1 - offsets])
    mode_index = lax.broadcasted_iota(jnp.int32, (size, 6), 0)
    phase_index = mode_index * (2 * cells[None, :] + 1) % (4 * live)
    count = live.astype(jnp.float32)
    radians = jnp.pi * phase_index.astype(jnp.float32) / (2.0 * count)
    norm_factor = jnp.where(mode_index == 0, jnp.sqrt(1.0 / count), jnp.sqrt(2.0 / count))
    return jnp.where(mode_index < live, norm_factor * jnp.cos(radians), jnp.float32(0.0))


def local(modes_now, modes_prev, extents):
    modes = modes_now[0]
    earlier = modes_prev[0]
    extent = extents[0]
    rows_y = modes.shape[0]
    size_z = modes.shape[1]
    size_x = modes.shape[2]
    size_y = rows_y * lax.axis_size("pencil")
    table_z = cosine_table(size_z, size_z)
    table_y = cosine_table(size_y, size_y)
    table_x = cosine_table(extent, size_x)
    columns = face_columns(extent, size_x)
    domain = lax.axis_index("dom")
    domains = lax.axis_size("dom")
    along_z = jnp.einsum("bck,cz->bzk", modes, table_z, precision=HIGH)
    along_y = jnp.einsum(
        "yzk,ya->zak",
        lax.all_to_all(along_z, "pencil", split_axis=1, concat_axis=0, tiled=True),
        table_y,
        precision=HIGH,
    )
    field = jnp.einsum("zyk,kx->zyx", along_y, table_x, precision=HIGH)
    rims = jnp.einsum("kl,bck->lbc", columns, modes, precision=HIGH)
    lower_rim, upper_rim = rims[:3], rims[3:]
    from_lower = from_behind(upper_rim, "dom", 1)
    from_upper = from_behind(lower_rim, "dom", -1)
    lower_force = face_forcing(lower_rim, from_lower) * (domain > 0).astype(jnp.float32)
    upper_force = face_forcing(upper_rim, from_upper) * (domain < domains - 1).astype(jnp.float32)
    layers = jnp.concatenate([lower_force, upper_force], axis=0)
    forcing = jnp.einsum("lbc,kl->bck", layers, columns, precision=HIGH)
    ky_start = lax.axis_index("pencil") * rows_y
    advanced = advance_modes(modes, earlier, forcing, extent, ky_start, size_y, size_z)
    return (field[None], advanced[None])


def solution(mesh):
    return jax.shard_map(
        local,
        mesh=mesh,
        in_specs=(P("dom", "pencil", None, None), P("dom", "pencil", None, None), P("dom")),
        out_specs=(P("dom", "pencil", None, None), P("dom", "pencil", None, None)),
        check_vma=False,
    )
```

```python
import functools

import jax
import jax.numpy as jnp
import numpy as np
from jax import lax
from jax.experimental import pallas as pl
from jax.experimental.pallas import tpu as pltpu
from jax.sharding import PartitionSpec as P

COEF_ONE = 1.5
COEF_TWO = -0.15
COEF_THREE = 1.0 / 90.0
STEP_DT = 0.5
SINC_SERIES = (1.0, -1.0 / 6, 1.0 / 120, -1.0 / 5040, 1.0 / 362880, -1.0 / 39916800, 1.0 / 6227020800, -1.0 / 1307674368000)
MESH = pl.DeviceIdType.MESH
BF16 = jnp.bfloat16
F32 = jnp.float32

NX, NY = 4, 8
NP = NX * NY
KY = 4
ZB = 16
GX, GY, GZ = 128, 128, 512
ROWS = KY * ZB
PAIRS = ((1, 7), (2, 6), (3, 5), (4, 0))


def split(value):
    high = value.astype(BF16)
    return high, (value - high.astype(F32)).astype(BF16)


def dot3(a, b, dims=(((1,), (0,)), ((), ()))):
    mul = functools.partial(lax.dot_general, dimension_numbers=dims, preferred_element_type=F32)
    return mul(a[0], b[0]) + (mul(a[0], b[1]) + mul(a[1], b[0]))


def cosine(phase, count):
    turns = jnp.floor(phase / (4.0 * count))
    phase = phase - turns * (4.0 * count)
    angle = (jnp.abs(phase - 2.0 * count) - count) / count * (jnp.pi / 2.0)
    square = angle * angle
    series = jnp.full_like(square, SINC_SERIES[-1])
    for term in SINC_SERIES[-2::-1]:
        series = series * square + term
    return angle * series


def table(mode, cell, count, inside):
    scale = jnp.sqrt(jnp.where(mode == 0.0, 1.0, 2.0) / count)
    return jnp.where(inside, scale * cosine(mode * (2.0 * cell + 1.0), count), 0.0)


def exchange_kernel(
    modes_hbm, prev_hbm, extent_ref, tzh_hbm, tzl_hbm, recv, next_hbm,
    modes, prev, tzh, tzl, high, low, send, rims, rim_out, from_lower, from_upper, nxt,
    in_sem, send_sem, recv_sem, rim_sem, out_sem,
):
    dom = lax.axis_index("dom")
    doms = lax.axis_size("dom")
    me = lax.axis_index("pencil")
    my_x, my_y = me // NY, me % NY
    above, below = (dom + 1) % doms, (dom + doms - 1) % doms

    loads = [
        pltpu.make_async_copy(modes_hbm, modes, in_sem.at[0]),
        pltpu.make_async_copy(tzh_hbm, tzh, in_sem.at[1]),
        pltpu.make_async_copy(tzl_hbm, tzl, in_sem.at[2]),
        pltpu.make_async_copy(prev_hbm, prev, in_sem.at[3]),
    ]
    for load in loads:
        load.start()

    barrier = pltpu.get_barrier_semaphore()

    def signal(i, carry):
        pl.semaphore_signal(barrier, inc=1, device_id={"pencil": (me + i) % NP}, device_id_type=MESH)
        return carry

    lax.fori_loop(1, NP, signal, 0)
    for other in (above, below):
        pl.semaphore_signal(barrier, inc=1, device_id={"dom": other}, device_id_type=MESH)

    count = jnp.full((8, GX), extent_ref[0, 0]).astype(F32)
    count_x = jnp.concatenate([count] * (GX // 8), axis=0)
    mode = lax.broadcasted_iota(jnp.int32, (GX, GX), 0).astype(F32)
    cell = lax.broadcasted_iota(jnp.int32, (GX, GX), 1).astype(F32)
    table_x = split(table(mode, cell, count_x, (mode < count_x) & (cell < count_x)))

    row = lax.broadcasted_iota(jnp.int32, (8, GX), 0).astype(F32)
    lane = lax.broadcasted_iota(jnp.int32, (8, GX), 1).astype(F32)
    upper = row >= 3.0
    layer = jnp.where(upper, row - 3.0, row)
    live = (lane < count) & (row < 6.0)

    def face(offset, is_upper):
        return table(lane, jnp.where(is_upper, count - 1.0 - offset, offset), count, live)

    own = face(layer, upper)
    swapped = face(layer, jnp.logical_not(upper))
    weights = ((COEF_ONE, COEF_TWO, COEF_THREE), (COEF_TWO, COEF_THREE, 0.0), (COEF_THREE, 0.0, 0.0))
    spread = jnp.zeros((8, GX), F32)
    for offset in range(3):
        factor = jnp.zeros((8, GX), F32)
        for m in range(3):
            factor = jnp.where(layer == float(m), weights[offset][m], factor)
        spread += factor * face(jnp.full((8, GX), float(offset)), upper)
    has_lower = jnp.where(dom > 0, 1.0, 0.0)
    has_upper = jnp.where(dom < doms - 1, 1.0, 0.0)
    spread = spread * jnp.where(upper, has_upper, has_lower)

    loads[0].wait()
    for ky in range(KY):
        h, l = split(modes[ky])
        high[:, ky * GX : (ky + 1) * GX] = h
        low[:, ky * GX : (ky + 1) * GX] = l
    loads[1].wait()
    loads[2].wait()

    def make_pair(chunk):
        starts = [((my_y + dy) % NY) for dy in PAIRS[chunk]]
        th = jnp.concatenate([tzh[y] for y in starts], axis=0)
        tl = jnp.concatenate([tzl[y] for y in starts], axis=0)
        along_z = dot3((th, tl), (high[...], low[...]))
        along_z = jnp.concatenate([along_z[:, ky * GX : (ky + 1) * GX] for ky in range(KY)], axis=0)
        along_x = dot3(split(along_z), table_x)
        for ky in range(KY):
            for half in range(2):
                for x in range(NX):
                    begin = ky * 2 * NX * ZB + (half * NX + x) * ZB
                    send[(2 * chunk + half) * NX + x, pl.ds(ky, ZB, stride=KY), :] = along_x[begin : begin + ZB]

    def transfer(slot_half, dx, dy):
        x, y = (my_x + dx) % NX, (my_y + dy) % NY
        index = dx * NY + dy
        return pltpu.make_async_remote_copy(
            src_ref=send.at[slot_half * NX + x],
            dst_ref=recv.at[me],
            send_sem=send_sem.at[index],
            recv_sem=recv_sem.at[index],
            device_id={"pencil": x * NY + y},
            device_id_type=MESH,
        )

    keep = pltpu.make_async_copy(send.at[7 * NX + my_x], recv.at[me], send_sem.at[0])

    def send_pair(chunk):
        for half in range(2):
            dy = PAIRS[chunk][half]
            first = 1 if dy == 0 else 0

            def go(dx, carry):
                transfer(2 * chunk + half, dx, dy).start()
                return carry

            lax.fori_loop(first, NX, go, 0)
            if dy == 0:
                keep.start()

    make_pair(0)
    pl.semaphore_wait(barrier, NP - 1 + 2)
    send_pair(0)

    columns = split(jnp.concatenate([own, swapped], axis=0))
    nt = (((1,), (1,)), ((), ()))
    for ky in range(KY):
        lanes = slice(ky * GX, (ky + 1) * GX)
        both = dot3(columns, (high[:, lanes], low[:, lanes]), nt)
        rims[ky] = both[:8]
        rim_out[ky] = both[8:]
    to_above = pltpu.make_async_remote_copy(
        src_ref=rim_out, dst_ref=from_lower, send_sem=rim_sem.at[0], recv_sem=rim_sem.at[1],
        device_id={"dom": above}, device_id_type=MESH,
    )
    to_below = pltpu.make_async_remote_copy(
        src_ref=rim_out, dst_ref=from_upper, send_sem=rim_sem.at[2], recv_sem=rim_sem.at[3],
        device_id={"dom": below}, device_id_type=MESH,
    )
    to_above.start()
    to_below.start()

    for chunk in range(1, 4):
        make_pair(chunk)
        send_pair(chunk)

    loads[3].wait()
    to_above.wait()
    to_below.wait()
    spread_h, spread_l = split(spread)
    spread3 = jnp.concatenate([spread_h, spread_h, spread_l, jnp.zeros_like(spread_h)], axis=0)
    half_step = (np.pi * STEP_DT / 2.0) ** 2
    part = 64
    mode_x = lax.broadcasted_iota(jnp.int32, (part, GX), 1).astype(F32)
    mode_z = lax.broadcasted_iota(jnp.int32, (part, GX), 0).astype(F32)
    count_p = jnp.concatenate([count] * (part // 8), axis=0)
    square_x = (mode_x / count_p) * (mode_x / count_p) * half_step
    is_upper = lax.broadcasted_iota(jnp.int32, (8, GZ), 0) >= 3
    for ky in range(KY):
        diff = jnp.where(is_upper, from_upper[ky], from_lower[ky]) - rims[ky]
        diff_h, diff_l = split(diff)
        diff3 = jnp.concatenate(
            [diff_h.astype(F32), diff_l.astype(F32), diff_h.astype(F32), jnp.zeros_like(diff)], axis=0
        )
        forcing = jnp.dot(diff3.T.astype(BF16), spread3, preferred_element_type=F32)
        mode_y = (me * KY + ky).astype(F32)
        square_xy = square_x + mode_y * mode_y * (half_step / (GY * GY))
        for begin in range(0, GZ, part):
            zs = mode_z + float(begin)
            square = square_xy + zs * zs * (half_step / (GZ * GZ))
            series = jnp.full_like(square, SINC_SERIES[-1])
            for term in SINC_SERIES[-2::-1]:
                series = series * square + term
            now = modes[ky, begin : begin + part, :]
            old = prev[ky, begin : begin + part, :]
            force = forcing[begin : begin + part, :]
            value = 2.0 * now - old + series * series * (STEP_DT * STEP_DT * force - 4.0 * square * now)
            nxt[ky, begin : begin + part, :] = jnp.where(mode_x < count_p, value, 0.0)
    out = pltpu.make_async_copy(nxt, next_hbm, out_sem)
    out.start()

    keep.wait()
    for chunk in range(4):
        for half in range(2):
            dy = PAIRS[chunk][half]

            def done(dx, carry):
                transfer(2 * chunk + half, dx, dy).wait()
                return carry

            lax.fori_loop(1 if dy == 0 else 0, NX, done, 0)
    out.wait()


def field_kernel(recv, th, tl, nxt, field, nxt_out, sem):
    out = pltpu.make_async_copy(nxt, nxt_out, sem)
    out.start()
    for q in range(0, 8, 2):
        parts = [recv[:, 8 * i : 8 * i + 8, :].reshape(NP * 8, GX) for i in (q, q + 1)]
        value = dot3((th[...], tl[...]), split(jnp.concatenate(parts, axis=1)))
        for i in range(2):
            for z in range(2):
                field[2 * (q + i) + z] = value[z * GY : (z + 1) * GY, i * GX : (i + 1) * GX]
    out.wait()


def host_split(value):
    value = value.astype(np.float32)
    high = value.astype(BF16)
    low = (value - high.astype(np.float32)).astype(BF16)
    return high, low


def host_table(size):
    mode = np.arange(size)[:, None]
    cell = np.arange(size)[None, :]
    scale = np.where(mode == 0, np.sqrt(1.0 / size), np.sqrt(2.0 / size))
    return scale * np.cos(np.pi * (mode * (2 * cell + 1) % (4 * size)) / (2.0 * size))


def tables():
    along_z = host_table(GZ).T
    along_z = along_z.reshape(NX, NY, ZB, GZ).transpose(1, 0, 2, 3).reshape(NY, NX * ZB, GZ)
    along_y = host_table(GY)
    pair = np.zeros((2, GY, NP, 2, KY))
    for z in range(2):
        pair[z, :, :, z, :] = along_y.T.reshape(GY, NP, KY)
    return host_split(along_z), host_split(pair.reshape(2 * GY, NP * 2 * KY))


def local(modes_now, modes_prev, extents):
    (tzh, tzl), (tyh, tyl) = tables()
    any_space = pl.BlockSpec(memory_space=pl.ANY)
    vmem = pl.BlockSpec(memory_space=pltpu.VMEM)
    recv, nxt = pl.pallas_call(
        exchange_kernel,
        out_shape=(
            jax.ShapeDtypeStruct((NP, ROWS, GX), F32),
            jax.ShapeDtypeStruct((KY, GZ, GX), F32),
        ),
        in_specs=[any_space, any_space, pl.BlockSpec(memory_space=pltpu.SMEM), any_space, any_space],
        out_specs=(any_space, any_space),
        scratch_shapes=[
            pltpu.VMEM((KY, GZ, GX), F32),
            pltpu.VMEM((KY, GZ, GX), F32),
            pltpu.VMEM((NY, NX * ZB, GZ), BF16),
            pltpu.VMEM((NY, NX * ZB, GZ), BF16),
            pltpu.VMEM((GZ, KY * GX), BF16),
            pltpu.VMEM((GZ, KY * GX), BF16),
            pltpu.VMEM((NP, ROWS, GX), F32),
            pltpu.VMEM((KY, 8, GZ), F32),
            pltpu.VMEM((KY, 8, GZ), F32),
            pltpu.VMEM((KY, 8, GZ), F32),
            pltpu.VMEM((KY, 8, GZ), F32),
            pltpu.VMEM((KY, GZ, GX), F32),
            pltpu.SemaphoreType.DMA((4,)),
            pltpu.SemaphoreType.DMA((NP,)),
            pltpu.SemaphoreType.DMA((NP,)),
            pltpu.SemaphoreType.DMA((4,)),
            pltpu.SemaphoreType.DMA,
        ],
        compiler_params=pltpu.CompilerParams(
            collective_id=0, has_side_effects=True, vmem_limit_bytes=24 * 1024 * 1024
        ),
        name="exchange",
    )(modes_now[0], modes_prev[0], extents.reshape(1, 1), tzh, tzl)
    field, advanced = pl.pallas_call(
        field_kernel,
        out_shape=(
            jax.ShapeDtypeStruct((ZB, GY, GX), F32),
            jax.ShapeDtypeStruct((KY, GZ, GX), F32),
        ),
        in_specs=[vmem, vmem, vmem, any_space],
        out_specs=(vmem, any_space),
        scratch_shapes=[pltpu.SemaphoreType.DMA],
        compiler_params=pltpu.CompilerParams(vmem_limit_bytes=24 * 1024 * 1024),
        name="field",
    )(recv, tyh, tyl, nxt)
    return (field[None], advanced[None])


def solution(mesh):
    return jax.shard_map(
        local,
        mesh=mesh,
        in_specs=(P("dom", "pencil", None, None), P("dom", "pencil", None, None), P("dom")),
        out_specs=(P("dom", "pencil", None, None), P("dom", "pencil", None, None)),
        check_vma=False,
    )
```

```python
import functools

import jax
import jax.numpy as jnp
import numpy as np
from jax import lax
from jax.experimental import pallas as pl
from jax.experimental.pallas import tpu as pltpu
from jax.sharding import PartitionSpec as P

COEF_ONE = 1.5
COEF_TWO = -0.15
COEF_THREE = 1.0 / 90.0
STEP_DT = 0.5
SINC_SERIES = (1.0, -1.0 / 6, 1.0 / 120, -1.0 / 5040, 1.0 / 362880, -1.0 / 39916800, 1.0 / 6227020800, -1.0 / 1307674368000)
MESH = pl.DeviceIdType.MESH
BF16 = jnp.bfloat16
F32 = jnp.float32

NX, NY = 4, 8
NP = NX * NY
KY = 4
ZB = 16
GX, GY, GZ = 128, 128, 512
ROWS = KY * ZB
PAIRS = ((1, 7), (0, 2), (6, 3), (5, 4))


def split(value):
    high = value.astype(BF16)
    return high, (value - high.astype(F32)).astype(BF16)


def dot3(a, b, dims=(((1,), (0,)), ((), ()))):
    mul = functools.partial(lax.dot_general, dimension_numbers=dims, preferred_element_type=F32)
    return mul(a[0], b[0]) + (mul(a[0], b[1]) + mul(a[1], b[0]))


def cosine(phase, count):
    turns = jnp.floor(phase / (4.0 * count))
    phase = phase - turns * (4.0 * count)
    angle = (jnp.abs(phase - 2.0 * count) - count) / count * (jnp.pi / 2.0)
    square = angle * angle
    series = jnp.full_like(square, SINC_SERIES[-1])
    for term in SINC_SERIES[-2::-1]:
        series = series * square + term
    return angle * series


def table(mode, cell, count, inside):
    scale = jnp.sqrt(jnp.where(mode == 0.0, 1.0, 2.0) / count)
    return jnp.where(inside, scale * cosine(mode * (2.0 * cell + 1.0), count), 0.0)


def exchange_kernel(
    modes_hbm, prev_hbm, extent_ref, tz_hbm, recv, next_out,
    modes, prev, tz, high, low, send, rims, rim_out, from_lower, from_upper,
    in_sem, tz_sem, send_sem, recv_sem, rim_sem, row_up, row_down, above_in,
):
    dom = lax.axis_index("dom")
    doms = lax.axis_size("dom")
    me = lax.axis_index("pencil")
    my_x, my_y = me // NY, me % NY
    y_up, y_down = my_x * NY + (my_y + 1) % NY, my_x * NY + (my_y + NY - 1) % NY

    barrier = pltpu.get_barrier_semaphore()
    row_peers = [((my_x + dx) % NX) * NY + my_y for dx in (2, 1, 3)]
    for other in row_peers + [y_up, y_down]:
        pl.semaphore_signal(barrier, inc=1, device_id={"pencil": other}, device_id_type=MESH)

    @pl.when(dom < doms - 1)
    def _():
        pl.semaphore_signal(barrier, inc=1, device_id={"dom": dom + 1}, device_id_type=MESH)

    load_modes = pltpu.make_async_copy(modes_hbm, modes, in_sem.at[0])
    load_prev = pltpu.make_async_copy(prev_hbm, prev, in_sem.at[1])
    load_tz = [
        pltpu.make_async_copy(tz_hbm.at[(my_y + dy) % NY], tz.at[slot], tz_sem.at[slot])
        for slot, dy in enumerate(sum(PAIRS, ()))
    ]
    load_modes.start()
    for load in load_tz:
        load.start()
    load_prev.start()

    count = jnp.full((8, GX), extent_ref[0, 0]).astype(F32)
    count_x = jnp.concatenate([count] * (GX // 8), axis=0)
    mode = lax.broadcasted_iota(jnp.int32, (GX, GX), 0).astype(F32)
    cell = lax.broadcasted_iota(jnp.int32, (GX, GX), 1).astype(F32)
    table_x = split(table(mode, cell, count_x, (mode < count_x) & (cell < count_x)))

    row = lax.broadcasted_iota(jnp.int32, (8, GX), 0).astype(F32)
    lane = lax.broadcasted_iota(jnp.int32, (8, GX), 1).astype(F32)
    upper = row >= 3.0
    layer = jnp.where(upper, row - 3.0, row)
    live = (lane < count) & (row < 6.0)

    def face(offset, is_upper):
        return table(lane, jnp.where(is_upper, count - 1.0 - offset, offset), count, live)

    own = face(layer, upper)
    swapped = face(layer, jnp.logical_not(upper))
    weights = ((COEF_ONE, COEF_TWO, COEF_THREE), (COEF_TWO, COEF_THREE, 0.0), (COEF_THREE, 0.0, 0.0))
    spread = jnp.zeros((8, GX), F32)
    for offset in range(3):
        factor = jnp.zeros((8, GX), F32)
        for m in range(3):
            factor = jnp.where(layer == float(m), weights[offset][m], factor)
        spread += factor * face(jnp.full((8, GX), float(offset)), upper)
    has_lower = jnp.where(dom > 0, 1.0, 0.0)
    has_upper = jnp.where(dom < doms - 1, 1.0, 0.0)
    spread = spread * jnp.where(upper, has_upper, has_lower)

    load_modes.wait()
    for ky in range(KY):
        h, l = split(modes[ky])
        high[:, ky * GX : (ky + 1) * GX] = h
        low[:, ky * GX : (ky + 1) * GX] = l

    def make_pair(chunk):
        slots = (2 * chunk, 2 * chunk + 1)
        for slot in slots:
            load_tz[slot].wait()
        th = jnp.concatenate([tz[slot, 0] for slot in slots], axis=0)
        tl = jnp.concatenate([tz[slot, 1] for slot in slots], axis=0)
        along_z = dot3((th, tl), (high[...], low[...]))
        along_z = jnp.concatenate([along_z[:, ky * GX : (ky + 1) * GX] for ky in range(KY)], axis=0)
        along_x = dot3(split(along_z), table_x)
        for ky in range(KY):
            for half in range(2):
                for x in range(NX):
                    begin = ky * 2 * NX * ZB + (half * NX + x) * ZB
                    send[slots[half] * NX + x, pl.ds(ky, ZB, stride=KY), :] = along_x[begin : begin + ZB]

    def transfer(slot, dy, dx):
        x, y = (my_x + dx) % NX, (my_y + dy) % NY
        index = dx * NY + dy
        return pltpu.make_async_remote_copy(
            src_ref=send.at[slot * NX + x],
            dst_ref=recv.at[me],
            send_sem=send_sem.at[index],
            recv_sem=recv_sem.at[index],
            device_id={"pencil": x * NY + y},
            device_id_type=MESH,
        )

    flat = sum(PAIRS, ())
    keep = pltpu.make_async_copy(send.at[flat.index(0) * NX + my_x], recv.at[me], send_sem.at[0])

    def send_row(dy):
        slot = flat.index(dy)

        def go(dx, carry):
            transfer(slot, dy, dx).start()
            return carry

        lax.fori_loop(1 if dy == 0 else 0, NX, go, 0)
        if dy == 0:
            keep.start()

    def tell(semaphore, other):
        pl.semaphore_signal(semaphore, inc=1, device_id={"pencil": other}, device_id_type=MESH)

    make_pair(0)
    pl.semaphore_wait(barrier, 5 + (dom + doms - 1) // doms)
    tell(row_up.at[0], y_down)
    tell(row_down.at[0], y_up)

    @pl.when(dom > 0)
    def _():
        pl.semaphore_signal(above_in, inc=1, device_id={"dom": dom - 1}, device_id_type=MESH)

    for step in range(4):
        pl.semaphore_wait(row_up.at[step], 1)
        if step < 3:
            tell(row_up.at[step + 1], y_down)
        send_row(step + 1)
        if step < 3:
            pl.semaphore_wait(row_down.at[step], 1)
            if step < 2:
                tell(row_down.at[step + 1], y_up)
            send_row(NY - step - 1)
        if step == 0:
            make_pair(1)
            send_row(0)
        if step < 2:
            make_pair(step + 2)

    columns = split(jnp.concatenate([own, swapped], axis=0))
    nt = (((1,), (1,)), ((), ()))
    for ky in range(KY):
        lanes = slice(ky * GX, (ky + 1) * GX)
        both = dot3(columns, (high[:, lanes], low[:, lanes]), nt)
        rims[ky] = both[:8]
        rim_out[ky] = both[8:]
    to_above = pltpu.make_async_remote_copy(
        src_ref=rim_out, dst_ref=from_lower, send_sem=rim_sem.at[0], recv_sem=rim_sem.at[1],
        device_id={"dom": dom + 1}, device_id_type=MESH,
    )
    to_below = pltpu.make_async_remote_copy(
        src_ref=rim_out, dst_ref=from_upper, send_sem=rim_sem.at[2], recv_sem=rim_sem.at[3],
        device_id={"dom": dom - 1}, device_id_type=MESH,
    )

    @pl.when(dom > 0)
    def _():
        to_below.start()

    @pl.when(dom < doms - 1)
    def _():
        pl.semaphore_wait(above_in, 1)
        to_above.start()

    load_prev.wait()

    @pl.when(dom > 0)
    def _():
        to_above.wait_recv()
        to_below.wait_send()

    @pl.when(dom == 0)
    def _():
        from_lower[...] = jnp.zeros_like(from_lower)

    @pl.when(dom < doms - 1)
    def _():
        to_below.wait_recv()
        to_above.wait_send()

    @pl.when(dom == doms - 1)
    def _():
        from_upper[...] = jnp.zeros_like(from_upper)

    spread_h, spread_l = split(spread)
    spread3 = jnp.concatenate([spread_h, spread_h, spread_l, jnp.zeros_like(spread_h)], axis=0)
    half_step = (np.pi * STEP_DT / 2.0) ** 2
    part = 64
    mode_x = lax.broadcasted_iota(jnp.int32, (part, GX), 1).astype(F32)
    mode_z = lax.broadcasted_iota(jnp.int32, (part, GX), 0).astype(F32)
    count_p = jnp.concatenate([count] * (part // 8), axis=0)
    square_x = (mode_x / count_p) * (mode_x / count_p) * half_step
    is_upper = lax.broadcasted_iota(jnp.int32, (8, GZ), 0) >= 3
    for ky in range(KY):
        diff = jnp.where(is_upper, from_upper[ky], from_lower[ky]) - rims[ky]
        diff_h, diff_l = split(diff)
        diff3 = jnp.concatenate(
            [diff_h.astype(F32), diff_l.astype(F32), diff_h.astype(F32), jnp.zeros_like(diff)], axis=0
        )
        forcing = jnp.dot(diff3.T.astype(BF16), spread3, preferred_element_type=F32)
        mode_y = (me * KY + ky).astype(F32)
        square_xy = square_x + mode_y * mode_y * (half_step / (GY * GY))
        for begin in range(0, GZ, part):
            zs = mode_z + float(begin)
            square = square_xy + zs * zs * (half_step / (GZ * GZ))
            series = jnp.full_like(square, SINC_SERIES[-1])
            for term in SINC_SERIES[-2::-1]:
                series = series * square + term
            now = modes[ky, begin : begin + part, :]
            old = prev[ky, begin : begin + part, :]
            force = forcing[begin : begin + part, :]
            value = 2.0 * now - old + series * series * (STEP_DT * STEP_DT * force - 4.0 * square * now)
            next_out[ky, begin : begin + part, :] = jnp.where(mode_x < count_p, value, 0.0)

    keep.wait()
    for dy in flat:
        slot = flat.index(dy)

        def done(dx, carry):
            transfer(slot, dy, dx).wait()
            return carry

        lax.fori_loop(1 if dy == 0 else 0, NX, done, 0)


def field_kernel(recv, th, tl, nxt, field_out, nxt_out, field, sem):
    outs = [pltpu.make_async_copy(nxt, nxt_out, sem.at[4])]
    outs[0].start()
    for step in range(4):
        parts = [recv[:, 8 * q : 8 * q + 8, :].reshape(NP * 8, GX) for q in (2 * step, 2 * step + 1)]
        value = dot3((th[...], tl[...]), split(jnp.concatenate(parts, axis=1)))
        for i in range(2):
            for z in range(2):
                field[4 * step + 2 * i + z] = value[z * GY : (z + 1) * GY, i * GX : (i + 1) * GX]
        part = pl.ds(4 * step, 4)
        outs.append(pltpu.make_async_copy(field.at[part], field_out.at[part], sem.at[step]))
        outs[-1].start()
    for out in outs:
        out.wait()


def host_split(value):
    value = value.astype(np.float32)
    high = value.astype(BF16)
    low = (value - high.astype(np.float32)).astype(BF16)
    return high, low


def host_table(size):
    mode = np.arange(size)[:, None]
    cell = np.arange(size)[None, :]
    scale = np.where(mode == 0, np.sqrt(1.0 / size), np.sqrt(2.0 / size))
    return scale * np.cos(np.pi * (mode * (2 * cell + 1) % (4 * size)) / (2.0 * size))


def tables():
    along_z = host_table(GZ).T
    along_z = along_z.reshape(NX, NY, ZB, GZ).transpose(1, 0, 2, 3).reshape(NY, NX * ZB, GZ)
    along_y = host_table(GY)
    pair = np.zeros((2, GY, NP, 2, KY))
    for z in range(2):
        pair[z, :, :, z, :] = along_y.T.reshape(GY, NP, KY)
    return host_split(along_z), host_split(pair.reshape(2 * GY, NP * 2 * KY))


def local(modes_now, modes_prev, extents):
    (tzh, tzl), (tyh, tyl) = tables()
    tz = np.stack([tzh, tzl], axis=1)
    hbm = pl.BlockSpec(memory_space=pltpu.HBM)
    vmem = pl.BlockSpec(memory_space=pltpu.VMEM)
    recv, nxt = pl.pallas_call(
        exchange_kernel,
        out_shape=(
            jax.ShapeDtypeStruct((NP, ROWS, GX), F32),
            jax.ShapeDtypeStruct((KY, GZ, GX), F32),
        ),
        in_specs=[hbm, hbm, pl.BlockSpec(memory_space=pltpu.SMEM), hbm],
        out_specs=(vmem, vmem),
        scratch_shapes=[
            pltpu.VMEM((KY, GZ, GX), F32),
            pltpu.VMEM((KY, GZ, GX), F32),
            pltpu.VMEM((NY, 2, NX * ZB, GZ), BF16),
            pltpu.VMEM((GZ, KY * GX), BF16),
            pltpu.VMEM((GZ, KY * GX), BF16),
            pltpu.VMEM((NP, ROWS, GX), F32),
            pltpu.VMEM((KY, 8, GZ), F32),
            pltpu.VMEM((KY, 8, GZ), F32),
            pltpu.VMEM((KY, 8, GZ), F32),
            pltpu.VMEM((KY, 8, GZ), F32),
            pltpu.SemaphoreType.DMA((2,)),
            pltpu.SemaphoreType.DMA((NY,)),
            pltpu.SemaphoreType.DMA((NP,)),
            pltpu.SemaphoreType.DMA((NP,)),
            pltpu.SemaphoreType.DMA((4,)),
            pltpu.SemaphoreType.REGULAR((4,)),
            pltpu.SemaphoreType.REGULAR((3,)),
            pltpu.SemaphoreType.REGULAR,
        ],
        compiler_params=pltpu.CompilerParams(
            collective_id=0, has_side_effects=True, vmem_limit_bytes=24 * 1024 * 1024
        ),
        name="exchange",
    )(*[pltpu.with_memory_space_constraint(v, pltpu.HBM) for v in (modes_now[0], modes_prev[0])], extents.reshape(1, 1), pltpu.with_memory_space_constraint(jnp.asarray(tz), pltpu.HBM))
    field, advanced = pl.pallas_call(
        field_kernel,
        out_shape=(
            jax.ShapeDtypeStruct((ZB, GY, GX), F32),
            jax.ShapeDtypeStruct((KY, GZ, GX), F32),
        ),
        in_specs=[vmem, vmem, vmem, vmem],
        out_specs=(hbm, hbm),
        scratch_shapes=[pltpu.VMEM((ZB, GY, GX), F32), pltpu.SemaphoreType.DMA((5,))],
        compiler_params=pltpu.CompilerParams(vmem_limit_bytes=24 * 1024 * 1024),
        name="field",
    )(recv, tyh, tyl, nxt)
    return (field[None], advanced[None])


def solution(mesh):
    return jax.shard_map(
        local,
        mesh=mesh,
        in_specs=(P("dom", "pencil", None, None), P("dom", "pencil", None, None), P("dom")),
        out_specs=(P("dom", "pencil", None, None), P("dom", "pencil", None, None)),
        check_vma=False,
    )
```

```python
import functools

import jax
import jax.numpy as jnp
import numpy as np
from jax import lax
from jax.experimental import pallas as pl
from jax.experimental.pallas import tpu as pltpu
from jax.sharding import PartitionSpec as P

COEF_ONE = 1.5
COEF_TWO = -0.15
COEF_THREE = 1.0 / 90.0
STEP_DT = 0.5
SINC_SERIES = (1.0, -1.0 / 6, 1.0 / 120, -1.0 / 5040, 1.0 / 362880, -1.0 / 39916800, 1.0 / 6227020800, -1.0 / 1307674368000)
MESH = pl.DeviceIdType.MESH
BF16 = jnp.bfloat16
F32 = jnp.float32

NX, NY = 4, 8
NP = NX * NY
KY = 4
ZB = 16
GX, GY, GZ = 128, 128, 512
ROWS = KY * ZB
PAIRS = ((1, 7), (2, 6), (4, 3), (5, 0))
ORDER = ((1, (2, 1, 3)), (7, (2, 1, 3)), (2, (2, 1, 3, 0)), (6, (2, 1, 3, 0)), (4, (2, 1, 3, 0)), (3, (2, 1, 3, 0)), (5, (2, 1, 3, 0)), (0, (2, 1, 3)), (1, (0,)), (7, (0,)))


def split(value):
    high = value.astype(BF16)
    return high, (value - high.astype(F32)).astype(BF16)


def dot3(a, b, dims=(((1,), (0,)), ((), ()))):
    mul = functools.partial(lax.dot_general, dimension_numbers=dims, preferred_element_type=F32)
    return mul(a[0], b[0]) + (mul(a[0], b[1]) + mul(a[1], b[0]))


def cosine(phase, count):
    turns = jnp.floor(phase / (4.0 * count))
    phase = phase - turns * (4.0 * count)
    angle = (jnp.abs(phase - 2.0 * count) - count) / count * (jnp.pi / 2.0)
    square = angle * angle
    series = jnp.full_like(square, SINC_SERIES[-1])
    for term in SINC_SERIES[-2::-1]:
        series = series * square + term
    return angle * series


def table(mode, cell, count, inside):
    scale = jnp.sqrt(jnp.where(mode == 0.0, 1.0, 2.0) / count)
    return jnp.where(inside, scale * cosine(mode * (2.0 * cell + 1.0), count), 0.0)


def exchange_kernel(
    modes_hbm, prev_hbm, extent_ref, tz_hbm, recv, next_out,
    modes, prev, tz, high, low, send, rims, rim_out, from_lower, from_upper,
    in_sem, tz_sem, send_sem, recv_sem, rim_sem, row_up, row_down, above_in,
):
    dom = lax.axis_index("dom")
    doms = lax.axis_size("dom")
    me = lax.axis_index("pencil")
    my_x, my_y = me // NY, me % NY
    y_up, y_down = my_x * NY + (my_y + 1) % NY, my_x * NY + (my_y + NY - 1) % NY

    barrier = pltpu.get_barrier_semaphore()
    row_peers = [((my_x + dx) % NX) * NY + my_y for dx in (2, 1, 3)]
    for other in row_peers + [y_up, y_down]:
        pl.semaphore_signal(barrier, inc=1, device_id={"pencil": other}, device_id_type=MESH)

    @pl.when(dom < doms - 1)
    def _():
        pl.semaphore_signal(barrier, inc=1, device_id={"dom": dom + 1}, device_id_type=MESH)

    halves = [pl.ds(0, GZ // 2), pl.ds(GZ // 2, GZ // 2)]
    load_modes = [
        pltpu.make_async_copy(modes_hbm.at[:, kz], modes.at[:, kz], in_sem.at[i]) for i, kz in enumerate(halves)
    ]
    load_prev = pltpu.make_async_copy(prev_hbm, prev, in_sem.at[2])
    load_tz = [
        pltpu.make_async_copy(tz_hbm.at[(my_y + dy) % NY], tz.at[slot], tz_sem.at[slot])
        for slot, dy in enumerate(sum(PAIRS, ()))
    ]
    for load in [load_modes[0], load_tz[0], load_tz[1], load_modes[1]] + load_tz[2:] + [load_prev]:
        load.start()

    count = jnp.full((8, GX), extent_ref[0, 0]).astype(F32)
    count_x = jnp.concatenate([count] * (GX // 8), axis=0)
    mode = lax.broadcasted_iota(jnp.int32, (GX, GX), 0).astype(F32)
    cell = lax.broadcasted_iota(jnp.int32, (GX, GX), 1).astype(F32)
    table_x = split(table(mode, cell, count_x, (mode < count_x) & (cell < count_x)))

    row = lax.broadcasted_iota(jnp.int32, (8, GX), 0).astype(F32)
    lane = lax.broadcasted_iota(jnp.int32, (8, GX), 1).astype(F32)
    upper = row >= 3.0
    layer = jnp.where(upper, row - 3.0, row)
    live = (lane < count) & (row < 6.0)

    def face(offset, is_upper):
        return table(lane, jnp.where(is_upper, count - 1.0 - offset, offset), count, live)

    own = face(layer, upper)
    swapped = face(layer, jnp.logical_not(upper))
    weights = ((COEF_ONE, COEF_TWO, COEF_THREE), (COEF_TWO, COEF_THREE, 0.0), (COEF_THREE, 0.0, 0.0))
    spread = jnp.zeros((8, GX), F32)
    for offset in range(3):
        factor = jnp.zeros((8, GX), F32)
        for m in range(3):
            factor = jnp.where(layer == float(m), weights[offset][m], factor)
        spread += factor * face(jnp.full((8, GX), float(offset)), upper)
    has_lower = jnp.where(dom > 0, 1.0, 0.0)
    has_upper = jnp.where(dom < doms - 1, 1.0, 0.0)
    spread = spread * jnp.where(upper, has_upper, has_lower)

    def along_z(slots, kz):
        th = jnp.concatenate([tz[slot, 0, :, kz] for slot in slots], axis=0)
        tl = jnp.concatenate([tz[slot, 1, :, kz] for slot in slots], axis=0)
        return dot3((th, tl), (high[kz, :], low[kz, :]))

    def finish(slots, value):
        value = jnp.concatenate([value[:, ky * GX : (ky + 1) * GX] for ky in range(KY)], axis=0)
        value = dot3(split(value), table_x)
        for half in range(2):
            for ky in range(KY):
                for x in range(NX):
                    begin = ky * 2 * NX * ZB + (half * NX + x) * ZB
                    send[slots[half] * NX + x, pl.ds(ky, ZB, stride=KY), :] = value[begin : begin + ZB]

    def make_pair(chunk):
        slots = (2 * chunk, 2 * chunk + 1)
        for slot in slots:
            load_tz[slot].wait()
        finish(slots, along_z(slots, slice(0, GZ)))

    load_tz[0].wait()
    load_tz[1].wait()
    first = jnp.zeros((2 * NX * ZB, KY * GX), F32)
    for i in range(2):
        load_modes[i].wait()
        kz = slice(i * GZ // 2, (i + 1) * GZ // 2)
        for ky in range(KY):
            h, l = split(modes[ky, kz, :])
            high[kz, ky * GX : (ky + 1) * GX] = h
            low[kz, ky * GX : (ky + 1) * GX] = l
        first += along_z((0, 1), kz)
    finish((0, 1), first)
    def transfer(slot, dy, dx):
        x, y = (my_x + dx) % NX, (my_y + dy) % NY
        return pltpu.make_async_remote_copy(
            src_ref=send.at[slot * NX + x],
            dst_ref=recv.at[me],
            send_sem=send_sem,
            recv_sem=recv_sem,
            device_id={"pencil": x * NY + y},
            device_id_type=MESH,
        )

    flat = sum(PAIRS, ())
    keep = pltpu.make_async_copy(send.at[flat.index(0) * NX + my_x], recv.at[me], in_sem.at[3])

    def tell(semaphore, other):
        pl.semaphore_signal(semaphore, inc=1, device_id={"pencil": other}, device_id_type=MESH)

    pl.semaphore_wait(barrier, 5 + (dom + doms - 1) // doms)
    tell(row_up.at[0], y_down)
    tell(row_down.at[0], y_up)

    @pl.when(dom > 0)
    def _():
        pl.semaphore_signal(above_in, inc=1, device_id={"dom": dom - 1}, device_id_type=MESH)

    known, made = 0, 1
    for dy, offsets in ORDER:
        while known < min(dy, NY - dy):
            pl.semaphore_wait(row_up.at[known], 1)
            if known < 3:
                tell(row_up.at[known + 1], y_down)
                pl.semaphore_wait(row_down.at[known], 1)
            if known < 2:
                tell(row_down.at[known + 1], y_up)
            known += 1
        while made <= flat.index(dy) // 2:
            make_pair(made)
            made += 1
        for dx in offsets:
            transfer(flat.index(dy), dy, dx).start()
    keep.start()

    columns = split(jnp.concatenate([own, swapped], axis=0))
    nt = (((1,), (1,)), ((), ()))
    for ky in range(KY):
        lanes = slice(ky * GX, (ky + 1) * GX)
        both = dot3(columns, (high[:, lanes], low[:, lanes]), nt)
        rims[ky] = both[:8]
        rim_out[ky] = both[8:]
    to_above = pltpu.make_async_remote_copy(
        src_ref=rim_out, dst_ref=from_lower, send_sem=rim_sem.at[0], recv_sem=rim_sem.at[1],
        device_id={"dom": dom + 1}, device_id_type=MESH,
    )
    to_below = pltpu.make_async_remote_copy(
        src_ref=rim_out, dst_ref=from_upper, send_sem=rim_sem.at[2], recv_sem=rim_sem.at[3],
        device_id={"dom": dom - 1}, device_id_type=MESH,
    )

    @pl.when(dom > 0)
    def _():
        to_below.start()

    @pl.when(dom < doms - 1)
    def _():
        pl.semaphore_wait(above_in, 1)
        to_above.start()

    load_prev.wait()

    @pl.when(dom > 0)
    def _():
        to_above.wait_recv()
        to_below.wait_send()

    @pl.when(dom == 0)
    def _():
        from_lower[...] = jnp.zeros_like(from_lower)

    @pl.when(dom < doms - 1)
    def _():
        to_below.wait_recv()
        to_above.wait_send()

    @pl.when(dom == doms - 1)
    def _():
        from_upper[...] = jnp.zeros_like(from_upper)

    spread_h, spread_l = split(spread)
    spread3 = jnp.concatenate([spread_h, spread_h, spread_l, jnp.zeros_like(spread_h)], axis=0)
    half_step = (np.pi * STEP_DT / 2.0) ** 2
    part = 64
    mode_x = lax.broadcasted_iota(jnp.int32, (part, GX), 1).astype(F32)
    mode_z = lax.broadcasted_iota(jnp.int32, (part, GX), 0).astype(F32)
    count_p = jnp.concatenate([count] * (part // 8), axis=0)
    square_x = (mode_x / count_p) * (mode_x / count_p) * half_step
    is_upper = lax.broadcasted_iota(jnp.int32, (8, GZ), 0) >= 3
    for ky in range(KY):
        diff = jnp.where(is_upper, from_upper[ky], from_lower[ky]) - rims[ky]
        diff_h, diff_l = split(diff)
        diff3 = jnp.concatenate(
            [diff_h.astype(F32), diff_l.astype(F32), diff_h.astype(F32), jnp.zeros_like(diff)], axis=0
        )
        forcing = jnp.dot(diff3.T.astype(BF16), spread3, preferred_element_type=F32)
        mode_y = (me * KY + ky).astype(F32)
        square_xy = square_x + mode_y * mode_y * (half_step / (GY * GY))
        for begin in range(0, GZ, part):
            zs = mode_z + float(begin)
            square = square_xy + zs * zs * (half_step / (GZ * GZ))
            series = jnp.full_like(square, SINC_SERIES[-1])
            for term in SINC_SERIES[-2::-1]:
                series = series * square + term
            now = modes[ky, begin : begin + part, :]
            old = prev[ky, begin : begin + part, :]
            force = forcing[begin : begin + part, :]
            value = 2.0 * now - old + series * series * (STEP_DT * STEP_DT * force - 4.0 * square * now)
            next_out[ky, begin : begin + part, :] = jnp.where(mode_x < count_p, value, 0.0)

    keep.wait()
    blocks = pl.ds(0, NP - 1)
    pltpu.make_async_remote_copy(
        src_ref=send.at[blocks], dst_ref=recv.at[blocks], send_sem=send_sem, recv_sem=recv_sem,
        device_id={"pencil": y_up}, device_id_type=MESH,
    ).wait()


def field_kernel(recv, th, tl, nxt, field_out, nxt_out, field, sem):
    outs = [pltpu.make_async_copy(nxt, nxt_out, sem.at[4])]
    outs[0].start()
    for step in range(4):
        parts = [recv[:, 8 * q : 8 * q + 8, :].reshape(NP * 8, GX) for q in (2 * step, 2 * step + 1)]
        value = dot3((th[...], tl[...]), split(jnp.concatenate(parts, axis=1)))
        for i in range(2):
            for z in range(2):
                field[4 * step + 2 * i + z] = value[z * GY : (z + 1) * GY, i * GX : (i + 1) * GX]
        part = pl.ds(4 * step, 4)
        outs.append(pltpu.make_async_copy(field.at[part], field_out.at[part], sem.at[step]))
        outs[-1].start()
    for out in outs:
        out.wait()


def host_split(value):
    value = value.astype(np.float32)
    high = value.astype(BF16)
    low = (value - high.astype(np.float32)).astype(BF16)
    return high, low


def host_table(size):
    mode = np.arange(size)[:, None]
    cell = np.arange(size)[None, :]
    scale = np.where(mode == 0, np.sqrt(1.0 / size), np.sqrt(2.0 / size))
    return scale * np.cos(np.pi * (mode * (2 * cell + 1) % (4 * size)) / (2.0 * size))


def tables():
    along_z = host_table(GZ).T
    along_z = along_z.reshape(NX, NY, ZB, GZ).transpose(1, 0, 2, 3).reshape(NY, NX * ZB, GZ)
    along_y = host_table(GY)
    pair = np.zeros((2, GY, NP, 2, KY))
    for z in range(2):
        pair[z, :, :, z, :] = along_y.T.reshape(GY, NP, KY)
    return host_split(along_z), host_split(pair.reshape(2 * GY, NP * 2 * KY))


def in_hbm(value):
    return pltpu.with_memory_space_constraint(value, pltpu.HBM)


def local(modes_now, modes_prev, extents):
    (tzh, tzl), (tyh, tyl) = tables()
    tz = np.stack([tzh, tzl], axis=1)
    hbm = pl.BlockSpec(memory_space=pltpu.HBM)
    vmem = pl.BlockSpec(memory_space=pltpu.VMEM)
    recv, nxt = pl.pallas_call(
        exchange_kernel,
        out_shape=(
            jax.ShapeDtypeStruct((NP, ROWS, GX), F32),
            jax.ShapeDtypeStruct((KY, GZ, GX), F32),
        ),
        in_specs=[hbm, hbm, pl.BlockSpec(memory_space=pltpu.SMEM), hbm],
        out_specs=(vmem, vmem),
        scratch_shapes=[
            pltpu.VMEM((KY, GZ, GX), F32),
            pltpu.VMEM((KY, GZ, GX), F32),
            pltpu.VMEM((NY, 2, NX * ZB, GZ), BF16),
            pltpu.VMEM((GZ, KY * GX), BF16),
            pltpu.VMEM((GZ, KY * GX), BF16),
            pltpu.VMEM((NP, ROWS, GX), F32),
            pltpu.VMEM((KY, 8, GZ), F32),
            pltpu.VMEM((KY, 8, GZ), F32),
            pltpu.VMEM((KY, 8, GZ), F32),
            pltpu.VMEM((KY, 8, GZ), F32),
            pltpu.SemaphoreType.DMA((4,)),
            pltpu.SemaphoreType.DMA((NY,)),
            pltpu.SemaphoreType.DMA,
            pltpu.SemaphoreType.DMA,
            pltpu.SemaphoreType.DMA((4,)),
            pltpu.SemaphoreType.REGULAR((4,)),
            pltpu.SemaphoreType.REGULAR((3,)),
            pltpu.SemaphoreType.REGULAR,
        ],
        compiler_params=pltpu.CompilerParams(
            collective_id=0, has_side_effects=True, vmem_limit_bytes=24 * 1024 * 1024
        ),
        name="exchange",
    )(in_hbm(modes_now[0]), in_hbm(modes_prev[0]), extents.reshape(1, 1), in_hbm(jnp.asarray(tz)))
    field, advanced = pl.pallas_call(
        field_kernel,
        out_shape=(
            jax.ShapeDtypeStruct((ZB, GY, GX), F32),
            jax.ShapeDtypeStruct((KY, GZ, GX), F32),
        ),
        in_specs=[vmem, vmem, vmem, vmem],
        out_specs=(hbm, hbm),
        scratch_shapes=[pltpu.VMEM((ZB, GY, GX), F32), pltpu.SemaphoreType.DMA((5,))],
        compiler_params=pltpu.CompilerParams(vmem_limit_bytes=24 * 1024 * 1024),
        name="field",
    )(recv, tyh, tyl, nxt)
    return (field[None], advanced[None])


def solution(mesh):
    return jax.shard_map(
        local,
        mesh=mesh,
        in_specs=(P("dom", "pencil", None, None), P("dom", "pencil", None, None), P("dom")),
        out_specs=(P("dom", "pencil", None, None), P("dom", "pencil", None, None)),
        check_vma=False,
    )
```

```python
import functools

import jax
import jax.numpy as jnp
import numpy as np
from jax import lax
from jax.experimental import pallas as pl
from jax.experimental.pallas import tpu as pltpu
from jax.sharding import PartitionSpec as P

COEF_ONE = 1.5
COEF_TWO = -0.15
COEF_THREE = 1.0 / 90.0
STEP_DT = 0.5
SINC_SERIES = (1.0, -1.0 / 6, 1.0 / 120, -1.0 / 5040, 1.0 / 362880, -1.0 / 39916800, 1.0 / 6227020800, -1.0 / 1307674368000)
MESH = pl.DeviceIdType.MESH
BF16 = jnp.bfloat16
F32 = jnp.float32

NX, NY = 4, 8
NP = NX * NY
KY = 4
ZB = 16
GX, GY, GZ = 128, 128, 512
ROWS = KY * ZB
PAIRS = ((1, 7), (2, 6), (3, 5), (4, 0))
ORDER = ((1, (2, 1, 3)), (7, (2, 1, 3)), (2, (2, 1, 3, 0)), (6, (2, 1, 3, 0)), (3, (2, 1)), (5, (2, 1)), (4, (2, 1, 3, 0)), (3, (3, 0)), (5, (3, 0)), (0, (2, 1, 3)), (1, (0,)), (7, (0,)))


def split(value):
    high = value.astype(BF16)
    return high, (value - high.astype(F32)).astype(BF16)


def dot3(a, b, dims=(((1,), (0,)), ((), ()))):
    mul = functools.partial(lax.dot_general, dimension_numbers=dims, preferred_element_type=F32)
    return mul(a[0], b[0]) + (mul(a[0], b[1]) + mul(a[1], b[0]))


def cosine(phase, count):
    turns = jnp.floor(phase / (4.0 * count))
    phase = phase - turns * (4.0 * count)
    angle = (jnp.abs(phase - 2.0 * count) - count) / count * (jnp.pi / 2.0)
    square = angle * angle
    series = jnp.full_like(square, SINC_SERIES[-1])
    for term in SINC_SERIES[-2::-1]:
        series = series * square + term
    return angle * series


def table(mode, cell, count, inside):
    scale = jnp.sqrt(jnp.where(mode == 0.0, 1.0, 2.0) / count)
    return jnp.where(inside, scale * cosine(mode * (2.0 * cell + 1.0), count), 0.0)


def exchange_kernel(
    modes_hbm, prev_hbm, extent_ref, tz_hbm, recv, next_out,
    modes, prev, tz, high, low, send, rims, rim_out, from_lower, from_upper,
    in_sem, tz_sem, send_sem, recv_sem, rim_sem, row_up, row_down, above_in,
):
    dom = lax.axis_index("dom")
    doms = lax.axis_size("dom")
    me = lax.axis_index("pencil")
    my_x, my_y = me // NY, me % NY
    y_up, y_down = my_x * NY + (my_y + 1) % NY, my_x * NY + (my_y + NY - 1) % NY

    barrier = pltpu.get_barrier_semaphore()
    for dx, dy in [(0, 1), (0, 7), (2, 0), (1, 0), (3, 0), (2, 1), (2, 7), (1, 1), (1, 7), (3, 1), (3, 7)]:
        other = ((my_x + dx) % NX) * NY + (my_y + dy) % NY
        pl.semaphore_signal(barrier, inc=1, device_id={"pencil": other}, device_id_type=MESH)

    @pl.when(dom < doms - 1)
    def _():
        pl.semaphore_signal(barrier, inc=1, device_id={"dom": dom + 1}, device_id_type=MESH)

    halves = [pl.ds(0, GZ // 2), pl.ds(GZ // 2, GZ // 2)]
    load_modes = [
        pltpu.make_async_copy(modes_hbm.at[:, kz], modes.at[:, kz], in_sem.at[i]) for i, kz in enumerate(halves)
    ]
    load_prev = pltpu.make_async_copy(prev_hbm, prev, in_sem.at[2])
    load_tz = [
        pltpu.make_async_copy(tz_hbm.at[(my_y + dy) % NY], tz.at[slot], tz_sem.at[slot])
        for slot, dy in enumerate(sum(PAIRS, ()))
    ]
    for load in [load_modes[0], load_tz[0], load_tz[1], load_modes[1]] + load_tz[2:] + [load_prev]:
        load.start()

    count = jnp.full((8, GX), extent_ref[0, 0]).astype(F32)
    count_x = jnp.concatenate([count] * (GX // 8), axis=0)
    mode = lax.broadcasted_iota(jnp.int32, (GX, GX), 0).astype(F32)
    cell = lax.broadcasted_iota(jnp.int32, (GX, GX), 1).astype(F32)
    table_x = split(table(mode, cell, count_x, (mode < count_x) & (cell < count_x)))

    row = lax.broadcasted_iota(jnp.int32, (8, GX), 0).astype(F32)
    lane = lax.broadcasted_iota(jnp.int32, (8, GX), 1).astype(F32)
    upper = row >= 3.0
    layer = jnp.where(upper, row - 3.0, row)
    live = (lane < count) & (row < 6.0)

    def face(offset, is_upper):
        return table(lane, jnp.where(is_upper, count - 1.0 - offset, offset), count, live)

    own = face(layer, upper)
    swapped = face(layer, jnp.logical_not(upper))
    weights = ((COEF_ONE, COEF_TWO, COEF_THREE), (COEF_TWO, COEF_THREE, 0.0), (COEF_THREE, 0.0, 0.0))
    spread = jnp.zeros((8, GX), F32)
    for offset in range(3):
        factor = jnp.zeros((8, GX), F32)
        for m in range(3):
            factor = jnp.where(layer == float(m), weights[offset][m], factor)
        spread += factor * face(jnp.full((8, GX), float(offset)), upper)
    has_lower = jnp.where(dom > 0, 1.0, 0.0)
    has_upper = jnp.where(dom < doms - 1, 1.0, 0.0)
    spread = spread * jnp.where(upper, has_upper, has_lower)

    def along_z(slots, kz):
        th = jnp.concatenate([tz[slot, 0, :, kz] for slot in slots], axis=0)
        tl = jnp.concatenate([tz[slot, 1, :, kz] for slot in slots], axis=0)
        return dot3((th, tl), (high[kz, :], low[kz, :]))

    def finish(slots, value):
        value = jnp.concatenate([value[:, ky * GX : (ky + 1) * GX] for ky in range(KY)], axis=0)
        value = dot3(split(value), table_x)
        for half in range(2):
            for ky in range(KY):
                for x in range(NX):
                    begin = ky * 2 * NX * ZB + (half * NX + x) * ZB
                    send[slots[half] * NX + x, pl.ds(ky, ZB, stride=KY), :] = value[begin : begin + ZB]

    def make_pair(chunk):
        slots = (2 * chunk, 2 * chunk + 1)
        for slot in slots:
            load_tz[slot].wait()
        finish(slots, along_z(slots, slice(0, GZ)))

    load_tz[0].wait()
    load_tz[1].wait()
    first = jnp.zeros((2 * NX * ZB, KY * GX), F32)
    for i in range(2):
        load_modes[i].wait()
        kz = slice(i * GZ // 2, (i + 1) * GZ // 2)
        for ky in range(KY):
            h, l = split(modes[ky, kz, :])
            high[kz, ky * GX : (ky + 1) * GX] = h
            low[kz, ky * GX : (ky + 1) * GX] = l
        first += along_z((0, 1), kz)
    finish((0, 1), first)
    def transfer(slot, dy, dx):
        x, y = (my_x + dx) % NX, (my_y + dy) % NY
        return pltpu.make_async_remote_copy(
            src_ref=send.at[slot * NX + x],
            dst_ref=recv.at[me],
            send_sem=send_sem,
            recv_sem=recv_sem,
            device_id={"pencil": x * NY + y},
            device_id_type=MESH,
        )

    flat = sum(PAIRS, ())
    keep = pltpu.make_async_copy(send.at[flat.index(0) * NX + my_x], recv.at[me], in_sem.at[3])

    def tell(semaphore, other):
        pl.semaphore_signal(semaphore, inc=1, device_id={"pencil": other}, device_id_type=MESH)

    pl.semaphore_wait(barrier, 11 + (dom + doms - 1) // doms)
    tell(row_up.at[0], y_down)
    tell(row_down.at[0], y_up)

    @pl.when(dom > 0)
    def _():
        pl.semaphore_signal(above_in, inc=1, device_id={"dom": dom - 1}, device_id_type=MESH)

    known, made = 1, 1
    for dy, offsets in ORDER:
        while made <= flat.index(dy) // 2:
            make_pair(made)
            made += 1
        while known < min(dy, NY - dy):
            pl.semaphore_wait(row_up.at[known - 1], 1)
            if known < 3:
                tell(row_up.at[known], y_down)
                pl.semaphore_wait(row_down.at[known - 1], 1)
            if known < 2:
                tell(row_down.at[known], y_up)
            known += 1
        for dx in offsets:
            transfer(flat.index(dy), dy, dx).start()
    keep.start()

    columns = split(jnp.concatenate([own, swapped], axis=0))
    nt = (((1,), (1,)), ((), ()))
    for ky in range(KY):
        lanes = slice(ky * GX, (ky + 1) * GX)
        both = dot3(columns, (high[:, lanes], low[:, lanes]), nt)
        rims[ky] = both[:8]
        rim_out[ky] = both[8:]
    to_above = pltpu.make_async_remote_copy(
        src_ref=rim_out, dst_ref=from_lower, send_sem=rim_sem.at[0], recv_sem=rim_sem.at[1],
        device_id={"dom": dom + 1}, device_id_type=MESH,
    )
    to_below = pltpu.make_async_remote_copy(
        src_ref=rim_out, dst_ref=from_upper, send_sem=rim_sem.at[2], recv_sem=rim_sem.at[3],
        device_id={"dom": dom - 1}, device_id_type=MESH,
    )

    @pl.when(dom > 0)
    def _():
        to_below.start()

    @pl.when(dom < doms - 1)
    def _():
        pl.semaphore_wait(above_in, 1)
        to_above.start()

    load_prev.wait()

    @pl.when(dom > 0)
    def _():
        to_above.wait_recv()
        to_below.wait_send()

    @pl.when(dom == 0)
    def _():
        from_lower[...] = jnp.zeros_like(from_lower)

    @pl.when(dom < doms - 1)
    def _():
        to_below.wait_recv()
        to_above.wait_send()

    @pl.when(dom == doms - 1)
    def _():
        from_upper[...] = jnp.zeros_like(from_upper)

    spread_h, spread_l = split(spread)
    spread3 = jnp.concatenate([spread_h, spread_h, spread_l, jnp.zeros_like(spread_h)], axis=0)
    half_step = (np.pi * STEP_DT / 2.0) ** 2
    part = 64
    mode_x = lax.broadcasted_iota(jnp.int32, (part, GX), 1).astype(F32)
    mode_z = lax.broadcasted_iota(jnp.int32, (part, GX), 0).astype(F32)
    count_p = jnp.concatenate([count] * (part // 8), axis=0)
    square_x = (mode_x / count_p) * (mode_x / count_p) * half_step
    is_upper = lax.broadcasted_iota(jnp.int32, (8, GZ), 0) >= 3
    for ky in range(KY):
        diff = jnp.where(is_upper, from_upper[ky], from_lower[ky]) - rims[ky]
        diff_h, diff_l = split(diff)
        diff3 = jnp.concatenate(
            [diff_h.astype(F32), diff_l.astype(F32), diff_h.astype(F32), jnp.zeros_like(diff)], axis=0
        )
        forcing = jnp.dot(diff3.T.astype(BF16), spread3, preferred_element_type=F32)
        mode_y = (me * KY + ky).astype(F32)
        square_xy = square_x + mode_y * mode_y * (half_step / (GY * GY))
        for begin in range(0, GZ, part):
            zs = mode_z + float(begin)
            square = square_xy + zs * zs * (half_step / (GZ * GZ))
            series = jnp.full_like(square, SINC_SERIES[-1])
            for term in SINC_SERIES[-2::-1]:
                series = series * square + term
            now = modes[ky, begin : begin + part, :]
            old = prev[ky, begin : begin + part, :]
            force = forcing[begin : begin + part, :]
            value = 2.0 * now - old + series * series * (STEP_DT * STEP_DT * force - 4.0 * square * now)
            next_out[ky, begin : begin + part, :] = jnp.where(mode_x < count_p, value, 0.0)

    keep.wait()
    blocks = pl.ds(0, NP - 1)
    pltpu.make_async_remote_copy(
        src_ref=send.at[blocks], dst_ref=recv.at[blocks], send_sem=send_sem, recv_sem=recv_sem,
        device_id={"pencil": y_up}, device_id_type=MESH,
    ).wait()


def field_kernel(recv, th, tl, nxt, field_out, nxt_out, field, sem):
    outs = [pltpu.make_async_copy(nxt, nxt_out, sem.at[4])]
    outs[0].start()
    for step in range(4):
        parts = [recv[:, 8 * q : 8 * q + 8, :].reshape(NP * 8, GX) for q in (2 * step, 2 * step + 1)]
        value = dot3((th[...], tl[...]), split(jnp.concatenate(parts, axis=1)))
        for i in range(2):
            for z in range(2):
                field[4 * step + 2 * i + z] = value[z * GY : (z + 1) * GY, i * GX : (i + 1) * GX]
        part = pl.ds(4 * step, 4)
        outs.append(pltpu.make_async_copy(field.at[part], field_out.at[part], sem.at[step]))
        outs[-1].start()
    for out in outs:
        out.wait()


def host_split(value):
    value = value.astype(np.float32)
    high = value.astype(BF16)
    low = (value - high.astype(np.float32)).astype(BF16)
    return high, low


def host_table(size):
    mode = np.arange(size)[:, None]
    cell = np.arange(size)[None, :]
    scale = np.where(mode == 0, np.sqrt(1.0 / size), np.sqrt(2.0 / size))
    return scale * np.cos(np.pi * (mode * (2 * cell + 1) % (4 * size)) / (2.0 * size))


def tables():
    along_z = host_table(GZ).T
    along_z = along_z.reshape(NX, NY, ZB, GZ).transpose(1, 0, 2, 3).reshape(NY, NX * ZB, GZ)
    along_y = host_table(GY)
    pair = np.zeros((2, GY, NP, 2, KY))
    for z in range(2):
        pair[z, :, :, z, :] = along_y.T.reshape(GY, NP, KY)
    return host_split(along_z), host_split(pair.reshape(2 * GY, NP * 2 * KY))


def in_hbm(value):
    return pltpu.with_memory_space_constraint(value, pltpu.HBM)


def local(modes_now, modes_prev, extents):
    (tzh, tzl), (tyh, tyl) = tables()
    tz = np.stack([tzh, tzl], axis=1)
    hbm = pl.BlockSpec(memory_space=pltpu.HBM)
    vmem = pl.BlockSpec(memory_space=pltpu.VMEM)
    recv, nxt = pl.pallas_call(
        exchange_kernel,
        out_shape=(
            jax.ShapeDtypeStruct((NP, ROWS, GX), F32),
            jax.ShapeDtypeStruct((KY, GZ, GX), F32),
        ),
        in_specs=[hbm, hbm, pl.BlockSpec(memory_space=pltpu.SMEM), hbm],
        out_specs=(vmem, vmem),
        scratch_shapes=[
            pltpu.VMEM((KY, GZ, GX), F32),
            pltpu.VMEM((KY, GZ, GX), F32),
            pltpu.VMEM((NY, 2, NX * ZB, GZ), BF16),
            pltpu.VMEM((GZ, KY * GX), BF16),
            pltpu.VMEM((GZ, KY * GX), BF16),
            pltpu.VMEM((NP, ROWS, GX), F32),
            pltpu.VMEM((KY, 8, GZ), F32),
            pltpu.VMEM((KY, 8, GZ), F32),
            pltpu.VMEM((KY, 8, GZ), F32),
            pltpu.VMEM((KY, 8, GZ), F32),
            pltpu.SemaphoreType.DMA((4,)),
            pltpu.SemaphoreType.DMA((NY,)),
            pltpu.SemaphoreType.DMA,
            pltpu.SemaphoreType.DMA,
            pltpu.SemaphoreType.DMA((4,)),
            pltpu.SemaphoreType.REGULAR((3,)),
            pltpu.SemaphoreType.REGULAR((2,)),
            pltpu.SemaphoreType.REGULAR,
        ],
        compiler_params=pltpu.CompilerParams(
            collective_id=0, has_side_effects=True, vmem_limit_bytes=24 * 1024 * 1024
        ),
        name="exchange",
    )(in_hbm(modes_now[0]), in_hbm(modes_prev[0]), extents.reshape(1, 1), in_hbm(jnp.asarray(tz)))
    field, advanced = pl.pallas_call(
        field_kernel,
        out_shape=(
            jax.ShapeDtypeStruct((ZB, GY, GX), F32),
            jax.ShapeDtypeStruct((KY, GZ, GX), F32),
        ),
        in_specs=[vmem, vmem, vmem, vmem],
        out_specs=(hbm, hbm),
        scratch_shapes=[pltpu.VMEM((ZB, GY, GX), F32), pltpu.SemaphoreType.DMA((5,))],
        compiler_params=pltpu.CompilerParams(vmem_limit_bytes=24 * 1024 * 1024),
        name="field",
    )(recv, tyh, tyl, nxt)
    return (field[None], advanced[None])


def solution(mesh):
    return jax.shard_map(
        local,
        mesh=mesh,
        in_specs=(P("dom", "pencil", None, None), P("dom", "pencil", None, None), P("dom")),
        out_specs=(P("dom", "pencil", None, None), P("dom", "pencil", None, None)),
        check_vma=False,
    )
```

```python
import functools

import jax
import jax.numpy as jnp
import numpy as np
from jax import lax
from jax.experimental import pallas as pl
from jax.experimental.pallas import tpu as pltpu
from jax.sharding import PartitionSpec as P

COEF_ONE = 1.5
COEF_TWO = -0.15
COEF_THREE = 1.0 / 90.0
STEP_DT = 0.5
SINC_SERIES = (1.0, -1.0 / 6, 1.0 / 120, -1.0 / 5040, 1.0 / 362880, -1.0 / 39916800, 1.0 / 6227020800, -1.0 / 1307674368000)
MESH = pl.DeviceIdType.MESH
BF16 = jnp.bfloat16
F32 = jnp.float32

NX, NY = 4, 8
NP = NX * NY
KY = 4
ZB = 16
GX, GY, GZ = 128, 128, 512
ROWS = KY * ZB
PAIRS = ((1, 7), (2, 6), (3, 5), (4, 0))
ORDER = ((1, (2, 1, 3)), (7, (2, 1, 3)), (2, (2, 1, 3)), (6, (2, 1, 3)), (3, (2, 1)), (5, (2, 1)), (4, (2, 1, 3, 0)), (3, (3, 0)), (5, (3, 0)), (2, (0,)), (6, (0,)), (0, (2, 1, 3)), (1, (0,)), (7, (0,)))


def split(value):
    high = value.astype(BF16)
    return high, (value - high.astype(F32)).astype(BF16)


def dot3(a, b, dims=(((1,), (0,)), ((), ()))):
    mul = functools.partial(lax.dot_general, dimension_numbers=dims, preferred_element_type=F32)
    return mul(a[0], b[0]) + (mul(a[0], b[1]) + mul(a[1], b[0]))


def cosine(phase, count):
    turns = jnp.floor(phase / (4.0 * count))
    phase = phase - turns * (4.0 * count)
    angle = (jnp.abs(phase - 2.0 * count) - count) / count * (jnp.pi / 2.0)
    square = angle * angle
    series = jnp.full_like(square, SINC_SERIES[-1])
    for term in SINC_SERIES[-2::-1]:
        series = series * square + term
    return angle * series


def table(mode, cell, count, inside):
    scale = jnp.sqrt(jnp.where(mode == 0.0, 1.0, 2.0) / count)
    return jnp.where(inside, scale * cosine(mode * (2.0 * cell + 1.0), count), 0.0)


def exchange_kernel(
    modes_hbm, prev_hbm, extent_ref, tz_hbm, recv, next_out,
    modes, prev, tz, high, low, send, rims, rim_out, from_lower, from_upper,
    in_sem, tz_sem, send_sem, recv_sem, rim_sem, row_up, row_down, above_in,
):
    dom = lax.axis_index("dom")
    doms = lax.axis_size("dom")
    me = lax.axis_index("pencil")
    my_x, my_y = me // NY, me % NY
    y_up, y_down = my_x * NY + (my_y + 1) % NY, my_x * NY + (my_y + NY - 1) % NY

    barrier = pltpu.get_barrier_semaphore()
    for dx, dy in [(0, 1), (0, 7), (2, 0), (1, 0), (3, 0), (2, 1), (2, 7), (1, 1), (1, 7), (3, 1), (3, 7)]:
        other = ((my_x + dx) % NX) * NY + (my_y + dy) % NY
        pl.semaphore_signal(barrier, inc=1, device_id={"pencil": other}, device_id_type=MESH)

    @pl.when(dom < doms - 1)
    def _():
        pl.semaphore_signal(barrier, inc=1, device_id={"dom": dom + 1}, device_id_type=MESH)

    halves = [pl.ds(0, GZ // 2), pl.ds(GZ // 2, GZ // 2)]
    load_modes = [
        pltpu.make_async_copy(modes_hbm.at[:, kz], modes.at[:, kz], in_sem.at[i]) for i, kz in enumerate(halves)
    ]
    load_prev = pltpu.make_async_copy(prev_hbm, prev, in_sem.at[2])
    load_tz = [
        pltpu.make_async_copy(tz_hbm.at[(my_y + dy) % NY], tz.at[slot], tz_sem.at[slot])
        for slot, dy in enumerate(sum(PAIRS, ()))
    ]
    for load in [load_modes[0], load_tz[0], load_tz[1], load_modes[1]] + load_tz[2:] + [load_prev]:
        load.start()

    count = jnp.full((8, GX), extent_ref[0, 0]).astype(F32)
    count_x = jnp.concatenate([count] * (GX // 8), axis=0)
    mode = lax.broadcasted_iota(jnp.int32, (GX, GX), 0).astype(F32)
    cell = lax.broadcasted_iota(jnp.int32, (GX, GX), 1).astype(F32)
    table_x = split(table(mode, cell, count_x, (mode < count_x) & (cell < count_x)))

    row = lax.broadcasted_iota(jnp.int32, (8, GX), 0).astype(F32)
    lane = lax.broadcasted_iota(jnp.int32, (8, GX), 1).astype(F32)
    upper = row >= 3.0
    layer = jnp.where(upper, row - 3.0, row)
    live = (lane < count) & (row < 6.0)

    def face(offset, is_upper):
        return table(lane, jnp.where(is_upper, count - 1.0 - offset, offset), count, live)

    own = face(layer, upper)
    swapped = face(layer, jnp.logical_not(upper))
    weights = ((COEF_ONE, COEF_TWO, COEF_THREE), (COEF_TWO, COEF_THREE, 0.0), (COEF_THREE, 0.0, 0.0))
    spread = jnp.zeros((8, GX), F32)
    for offset in range(3):
        factor = jnp.zeros((8, GX), F32)
        for m in range(3):
            factor = jnp.where(layer == float(m), weights[offset][m], factor)
        spread += factor * face(jnp.full((8, GX), float(offset)), upper)
    has_lower = jnp.where(dom > 0, 1.0, 0.0)
    has_upper = jnp.where(dom < doms - 1, 1.0, 0.0)
    spread = spread * jnp.where(upper, has_upper, has_lower)

    def along_z(slots, kz):
        th = jnp.concatenate([tz[slot, 0, :, kz] for slot in slots], axis=0)
        tl = jnp.concatenate([tz[slot, 1, :, kz] for slot in slots], axis=0)
        return dot3((th, tl), (high[kz, :], low[kz, :]))

    def finish(slots, value):
        value = jnp.concatenate([value[:, ky * GX : (ky + 1) * GX] for ky in range(KY)], axis=0)
        value = dot3(split(value), table_x)
        for half in range(2):
            for ky in range(KY):
                for x in range(NX):
                    begin = ky * 2 * NX * ZB + (half * NX + x) * ZB
                    send[slots[half] * NX + x, pl.ds(ky, ZB, stride=KY), :] = value[begin : begin + ZB]

    def make_pair(chunk):
        slots = (2 * chunk, 2 * chunk + 1)
        for slot in slots:
            load_tz[slot].wait()
        finish(slots, along_z(slots, slice(0, GZ)))

    load_tz[0].wait()
    load_tz[1].wait()
    first = jnp.zeros((2 * NX * ZB, KY * GX), F32)
    for i in range(2):
        load_modes[i].wait()
        kz = slice(i * GZ // 2, (i + 1) * GZ // 2)
        for ky in range(KY):
            h, l = split(modes[ky, kz, :])
            high[kz, ky * GX : (ky + 1) * GX] = h
            low[kz, ky * GX : (ky + 1) * GX] = l
        first += along_z((0, 1), kz)
    finish((0, 1), first)
    def transfer(slot, dy, dx):
        x, y = (my_x + dx) % NX, (my_y + dy) % NY
        return pltpu.make_async_remote_copy(
            src_ref=send.at[slot * NX + x],
            dst_ref=recv.at[me],
            send_sem=send_sem,
            recv_sem=recv_sem,
            device_id={"pencil": x * NY + y},
            device_id_type=MESH,
        )

    flat = sum(PAIRS, ())
    keep = pltpu.make_async_copy(send.at[flat.index(0) * NX + my_x], recv.at[me], in_sem.at[3])

    def tell(semaphore, other):
        pl.semaphore_signal(semaphore, inc=1, device_id={"pencil": other}, device_id_type=MESH)

    pl.semaphore_wait(barrier, 11 + (dom + doms - 1) // doms)
    tell(row_up.at[0], y_down)
    tell(row_down.at[0], y_up)

    @pl.when(dom > 0)
    def _():
        pl.semaphore_signal(above_in, inc=1, device_id={"dom": dom - 1}, device_id_type=MESH)

    known, made = 1, 1
    for dy, offsets in ORDER:
        while made <= flat.index(dy) // 2:
            make_pair(made)
            made += 1
        while known < min(dy, NY - dy):
            pl.semaphore_wait(row_up.at[known - 1], 1)
            if known < 3:
                tell(row_up.at[known], y_down)
                pl.semaphore_wait(row_down.at[known - 1], 1)
            if known < 2:
                tell(row_down.at[known], y_up)
            known += 1
        for dx in offsets:
            transfer(flat.index(dy), dy, dx).start()
    keep.start()

    columns = split(jnp.concatenate([own, swapped], axis=0))
    nt = (((1,), (1,)), ((), ()))
    for ky in range(KY):
        lanes = slice(ky * GX, (ky + 1) * GX)
        both = dot3(columns, (high[:, lanes], low[:, lanes]), nt)
        rims[ky] = both[:8]
        rim_out[ky] = both[8:]
    to_above = pltpu.make_async_remote_copy(
        src_ref=rim_out, dst_ref=from_lower, send_sem=rim_sem.at[0], recv_sem=rim_sem.at[1],
        device_id={"dom": dom + 1}, device_id_type=MESH,
    )
    to_below = pltpu.make_async_remote_copy(
        src_ref=rim_out, dst_ref=from_upper, send_sem=rim_sem.at[2], recv_sem=rim_sem.at[3],
        device_id={"dom": dom - 1}, device_id_type=MESH,
    )

    @pl.when(dom > 0)
    def _():
        to_below.start()

    @pl.when(dom < doms - 1)
    def _():
        pl.semaphore_wait(above_in, 1)
        to_above.start()

    load_prev.wait()

    @pl.when(dom > 0)
    def _():
        to_above.wait_recv()
        to_below.wait_send()

    @pl.when(dom == 0)
    def _():
        from_lower[...] = jnp.zeros_like(from_lower)

    @pl.when(dom < doms - 1)
    def _():
        to_below.wait_recv()
        to_above.wait_send()

    @pl.when(dom == doms - 1)
    def _():
        from_upper[...] = jnp.zeros_like(from_upper)

    spread_h, spread_l = split(spread)
    spread3 = jnp.concatenate([spread_h, spread_h, spread_l, jnp.zeros_like(spread_h)], axis=0)
    half_step = (np.pi * STEP_DT / 2.0) ** 2
    part = 64
    mode_x = lax.broadcasted_iota(jnp.int32, (part, GX), 1).astype(F32)
    mode_z = lax.broadcasted_iota(jnp.int32, (part, GX), 0).astype(F32)
    count_p = jnp.concatenate([count] * (part // 8), axis=0)
    square_x = (mode_x / count_p) * (mode_x / count_p) * half_step
    is_upper = lax.broadcasted_iota(jnp.int32, (8, GZ), 0) >= 3
    for ky in range(KY):
        diff = jnp.where(is_upper, from_upper[ky], from_lower[ky]) - rims[ky]
        diff_h, diff_l = split(diff)
        diff3 = jnp.concatenate(
            [diff_h.astype(F32), diff_l.astype(F32), diff_h.astype(F32), jnp.zeros_like(diff)], axis=0
        )
        forcing = jnp.dot(diff3.T.astype(BF16), spread3, preferred_element_type=F32)
        mode_y = (me * KY + ky).astype(F32)
        square_xy = square_x + mode_y * mode_y * (half_step / (GY * GY))
        for begin in range(0, GZ, part):
            zs = mode_z + float(begin)
            square = square_xy + zs * zs * (half_step / (GZ * GZ))
            series = jnp.full_like(square, SINC_SERIES[-1])
            for term in SINC_SERIES[-2::-1]:
                series = series * square + term
            now = modes[ky, begin : begin + part, :]
            old = prev[ky, begin : begin + part, :]
            force = forcing[begin : begin + part, :]
            value = 2.0 * now - old + series * series * (STEP_DT * STEP_DT * force - 4.0 * square * now)
            next_out[ky, begin : begin + part, :] = jnp.where(mode_x < count_p, value, 0.0)

    keep.wait()
    blocks = pl.ds(0, NP - 1)
    pltpu.make_async_remote_copy(
        src_ref=send.at[blocks], dst_ref=recv.at[blocks], send_sem=send_sem, recv_sem=recv_sem,
        device_id={"pencil": y_up}, device_id_type=MESH,
    ).wait()


def field_kernel(recv, th, tl, nxt, field_out, nxt_out, field, sem):
    outs = [pltpu.make_async_copy(nxt, nxt_out, sem.at[4])]
    outs[0].start()
    for step in range(4):
        parts = [recv[:, 8 * q : 8 * q + 8, :].reshape(NP * 8, GX) for q in (2 * step, 2 * step + 1)]
        value = dot3((th[...], tl[...]), split(jnp.concatenate(parts, axis=1)))
        for i in range(2):
            for z in range(2):
                field[4 * step + 2 * i + z] = value[z * GY : (z + 1) * GY, i * GX : (i + 1) * GX]
        part = pl.ds(4 * step, 4)
        outs.append(pltpu.make_async_copy(field.at[part], field_out.at[part], sem.at[step]))
        outs[-1].start()
    for out in outs:
        out.wait()


def host_split(value):
    value = value.astype(np.float32)
    high = value.astype(BF16)
    low = (value - high.astype(np.float32)).astype(BF16)
    return high, low


def host_table(size):
    mode = np.arange(size)[:, None]
    cell = np.arange(size)[None, :]
    scale = np.where(mode == 0, np.sqrt(1.0 / size), np.sqrt(2.0 / size))
    return scale * np.cos(np.pi * (mode * (2 * cell + 1) % (4 * size)) / (2.0 * size))


def tables():
    along_z = host_table(GZ).T
    along_z = along_z.reshape(NX, NY, ZB, GZ).transpose(1, 0, 2, 3).reshape(NY, NX * ZB, GZ)
    along_y = host_table(GY)
    pair = np.zeros((2, GY, NP, 2, KY))
    for z in range(2):
        pair[z, :, :, z, :] = along_y.T.reshape(GY, NP, KY)
    return host_split(along_z), host_split(pair.reshape(2 * GY, NP * 2 * KY))


def in_hbm(value):
    return pltpu.with_memory_space_constraint(value, pltpu.HBM)


def local(modes_now, modes_prev, extents):
    (tzh, tzl), (tyh, tyl) = tables()
    tz = np.stack([tzh, tzl], axis=1)
    hbm = pl.BlockSpec(memory_space=pltpu.HBM)
    vmem = pl.BlockSpec(memory_space=pltpu.VMEM)
    recv, nxt = pl.pallas_call(
        exchange_kernel,
        out_shape=(
            jax.ShapeDtypeStruct((NP, ROWS, GX), F32),
            jax.ShapeDtypeStruct((KY, GZ, GX), F32),
        ),
        in_specs=[hbm, hbm, pl.BlockSpec(memory_space=pltpu.SMEM), hbm],
        out_specs=(vmem, vmem),
        scratch_shapes=[
            pltpu.VMEM((KY, GZ, GX), F32),
            pltpu.VMEM((KY, GZ, GX), F32),
            pltpu.VMEM((NY, 2, NX * ZB, GZ), BF16),
            pltpu.VMEM((GZ, KY * GX), BF16),
            pltpu.VMEM((GZ, KY * GX), BF16),
            pltpu.VMEM((NP, ROWS, GX), F32),
            pltpu.VMEM((KY, 8, GZ), F32),
            pltpu.VMEM((KY, 8, GZ), F32),
            pltpu.VMEM((KY, 8, GZ), F32),
            pltpu.VMEM((KY, 8, GZ), F32),
            pltpu.SemaphoreType.DMA((4,)),
            pltpu.SemaphoreType.DMA((NY,)),
            pltpu.SemaphoreType.DMA,
            pltpu.SemaphoreType.DMA,
            pltpu.SemaphoreType.DMA((4,)),
            pltpu.SemaphoreType.REGULAR((3,)),
            pltpu.SemaphoreType.REGULAR((2,)),
            pltpu.SemaphoreType.REGULAR,
        ],
        compiler_params=pltpu.CompilerParams(
            collective_id=0, has_side_effects=True, vmem_limit_bytes=24 * 1024 * 1024
        ),
        name="exchange",
    )(in_hbm(modes_now[0]), in_hbm(modes_prev[0]), extents.reshape(1, 1), in_hbm(jnp.asarray(tz)))
    field, advanced = pl.pallas_call(
        field_kernel,
        out_shape=(
            jax.ShapeDtypeStruct((ZB, GY, GX), F32),
            jax.ShapeDtypeStruct((KY, GZ, GX), F32),
        ),
        in_specs=[vmem, vmem, vmem, vmem],
        out_specs=(hbm, hbm),
        scratch_shapes=[pltpu.VMEM((ZB, GY, GX), F32), pltpu.SemaphoreType.DMA((5,))],
        compiler_params=pltpu.CompilerParams(vmem_limit_bytes=24 * 1024 * 1024),
        name="field",
    )(recv, tyh, tyl, nxt)
    return (field[None], advanced[None])


def solution(mesh):
    return jax.shard_map(
        local,
        mesh=mesh,
        in_specs=(P("dom", "pencil", None, None), P("dom", "pencil", None, None), P("dom")),
        out_specs=(P("dom", "pencil", None, None), P("dom", "pencil", None, None)),
        check_vma=False,
    )
```
